512 devices in a mesh: row: 32 (over y, z_lo, core), col: 16 (over x, z_hi).
Axes of the slice: x: 4, y: 4, z: 16 (z_hi: 4, z_lo: 4; z = z_hi * 4 + z_lo), core: 2. Of those that a mesh axis runs over, the one named last changes fastest.
Arguments:
- queries: bfloat16 [128, 1024, 1024], P('row', 'col'), may hold values from -5 to 5
- key_vectors: bfloat16 [128, 1024, 1024], P('row', 'col'), may hold values from -5 to 5
- values: bfloat16 [128, 1024, 1024], P('row', 'col'), may hold values from -6 to 6
- out_weight: bfloat16 [1024, 1024], replicated, may hold values from -0.1875 to 0.1875
Outputs:
- attended: bfloat16 [128, 1024, 1024], P('row', 'col')
The draws below stay inside these ranges and needn't reach their ends.
All inputs are finite; a program needn't handle non-finite values.
Results may differ from the reference program's by a relative error of at most 0.0095.
Values may be sent and summed in bfloat16 or wider, within the bound.
A program may use at most 64 MiB of HBM per device.

```python
import jax
import jax.numpy as jnp
from jax import lax

HEADS = 8
HEAD_DIM = 128
D = 1024
STRIDE = 1024
ROWS = 128


def draw_queries(key, part):
    key = jax.random.fold_in(key, 1)
    return jax.random.truncated_normal(key, -4.0, 4.0, (ROWS, STRIDE, D), jnp.float32).astype(jnp.bfloat16)


def draw_key_vectors(key, part):
    key = jax.random.fold_in(key, 2)
    return jax.random.truncated_normal(key, -4.0, 4.0, (ROWS, STRIDE, D), jnp.float32).astype(jnp.bfloat16)


def steps_of(stream_key, shape, split, least, high):
    loudness = 1.0
    for axis_at, shards_of in split:
        draws = jax.random.uniform(jax.random.fold_in(jax.random.fold_in(stream_key, 6), axis_at), (shards_of,), jnp.float32, least / len(split), high / len(split))
        loudness = loudness * jnp.repeat(jnp.exp(draws), shape[axis_at] // shards_of).reshape((-1,) + (1,) * (len(shape) - 1 - axis_at))
    return loudness


def normal_values(own_key, shape, scale, bound, pieces=(), kind=jnp.bfloat16):
    result = jax.random.normal(own_key, shape, jnp.float32) * scale
    if len(pieces) > 0:
        result = steps_of(own_key, shape, pieces, -0.22, 0.18) * result
    return jnp.clip(result, min=-bound, max=bound).astype(kind)


def setup_inputs(seed: int = 0) -> dict:
    keys = jax.random.split(jax.random.key(seed), 5)
    queries = draw_queries(jax.random.fold_in(keys[4], 71), 0)
    key_vectors = draw_key_vectors(jax.random.fold_in(keys[4], 71), 0)
    values = normal_values(keys[2], (ROWS, STRIDE, D), 1.0, 6.0, ((0, 32), (1, 16)))
    out_weight = normal_values(keys[3], (D, D), D ** -0.5, 0.1875)
    return dict(queries=queries, key_vectors=key_vectors, values=values, out_weight=out_weight)


masked_fill = -1.0e30


def reduce_set(summed, best, totals):
    floor_total = jnp.maximum(totals, 1.0)
    part = (summed / floor_total[..., None]).astype(jnp.bfloat16)
    level = (best + jnp.log(floor_total)).astype(jnp.bfloat16)
    return part, level


def row_sets(item):
    query_rows, key_rows, value_rows = item
    width = query_rows.shape[0]
    tri_mask = lax.broadcasted_iota(jnp.int32, (width, width), 0) >= lax.broadcasted_iota(jnp.int32, (width, width), 1)
    scores = jnp.einsum("jhd,khd->hjk", query_rows.astype(jnp.float32), key_rows.astype(jnp.float32)) * (HEAD_DIM ** -0.5)
    best = jnp.max(jnp.where(tri_mask[None], scores, masked_fill), axis=-1)
    weights = jnp.where(tri_mask[None], jnp.exp(scores - best[..., None]), 0.0)
    totals = jnp.sum(weights, axis=-1)
    summed = jnp.einsum("hjk,khd->jhd", weights.astype(jnp.bfloat16).astype(jnp.float32), value_rows.astype(jnp.float32))
    return reduce_set(summed, best.T, totals.T)


def column_sets(item):
    query_cols, key_cols, value_cols = item
    depth = query_cols.shape[1]
    lower_mask = lax.broadcasted_iota(jnp.int32, (depth, depth), 0) > lax.broadcasted_iota(jnp.int32, (depth, depth), 1)
    scores = jnp.einsum("crhd,cshd->chrs", query_cols.astype(jnp.float32), key_cols.astype(jnp.float32)) * (HEAD_DIM ** -0.5)
    best = jnp.max(jnp.where(lower_mask, scores, masked_fill), axis=-1)
    weights = jnp.where(lower_mask, jnp.exp(scores - best[..., None]), 0.0)
    totals = jnp.sum(weights, axis=-1)
    summed = jnp.einsum("chrs,cshd->crhd", weights.astype(jnp.bfloat16).astype(jnp.float32), value_cols.astype(jnp.float32))
    return reduce_set(summed, best.transpose(0, 2, 1), totals.transpose(0, 2, 1))


def reference(queries, key_vectors, values, out_weight):
    grid_rows, stride_len, width = queries.shape
    shape_four = (grid_rows, stride_len, HEADS, HEAD_DIM)
    query_four = queries.reshape(shape_four)
    key_four = key_vectors.reshape(shape_four)
    value_four = values.reshape(shape_four)
    row_part, row_level = lax.map(row_sets, (query_four, key_four, value_four))
    block = 64
    def by_columns(x):
        return x.transpose(1, 0, 2, 3).reshape(stride_len // block, block, grid_rows, HEADS, HEAD_DIM)
    col_part, col_level = lax.map(column_sets, (by_columns(query_four), by_columns(key_four), by_columns(value_four)))
    col_part = col_part.reshape(stride_len, grid_rows, HEADS, HEAD_DIM).transpose(1, 0, 2, 3)
    col_level = col_level.reshape(stride_len, grid_rows, HEADS).transpose(1, 0, 2)
    row_level = row_level.astype(jnp.float32)
    col_level = col_level.astype(jnp.float32)
    top = jnp.maximum(row_level, col_level)
    row_factor = jnp.exp(row_level - top)
    col_factor = jnp.exp(col_level - top)
    numer = row_factor[..., None] * row_part.astype(jnp.float32) + col_factor[..., None] * col_part.astype(jnp.float32)
    denom = row_factor + col_factor
    context = (numer / denom[..., None]).reshape(grid_rows * stride_len, width).astype(jnp.bfloat16)
    attended = jnp.dot(context, out_weight, preferred_element_type=jnp.float32).astype(jnp.bfloat16)
    return attended.reshape(grid_rows, stride_len, width)
```

```python
import jax
import jax.numpy as jnp
from jax import lax
from jax.experimental import pallas as pl
from jax.experimental.pallas import tpu as pltpu
from jax.sharding import PartitionSpec as P

HEADS = 8
HEAD_DIM = 128
SCALE = HEAD_DIM**-0.5
BATCHES = 2
PER = 4 // BATCHES
GROUPS = 2 + BATCHES
BLOCK = 256
MASKED = -1e30
MESH = pl.DeviceIdType.MESH
NT = (((1,), (1,)), ((), ()))


def device(x, y, z, core):
    return (y * 8 + lax.rem(z, 4) * 2 + core, x * 4 + lax.div(z, 4))


def loop(first, last, step):
    def run(i, carry):
        step(i)
        return carry

    lax.fori_loop(first, last, run, 0)


def kernel(
    q_in,
    k_in,
    v_in,
    out,
    home_q,
    home_k,
    home_v,
    row_q,
    row_k,
    row_v,
    col_q,
    col_k,
    col_v,
    row_part,
    row_level,
    col_part,
    col_level,
    home_row_part,
    home_row_level,
    home_col_part,
    home_col_level,
    home_context,
    wide_q,
    wide_k,
    wide_v,
    wide_o,
    in_send,
    in_recv,
    row_send,
    row_recv,
    col_send,
    col_recv,
    row_back_send,
    row_back_recv,
    col_back_send,
    col_back_recv,
    out_send,
    out_recv,
):
    at_row, at_col = lax.axis_index("row"), lax.axis_index("col")
    y, z_lo, core = lax.div(at_row, 8), lax.rem(lax.div(at_row, 2), 4), lax.rem(at_row, 2)
    x, z_hi = lax.div(at_col, 4), lax.rem(at_col, 4)
    z = z_hi * 4 + z_lo
    near = lax.div(z, 2)
    active = lax.rem(z, 2) == 0
    me = y * 2 + core

    def peer_x(other):
        return device(other, y, z, core)

    def peer_yc(other):
        return device(x, lax.div(other, 2), z, lax.rem(other, 2))

    def peer_z(other):
        return device(x, y, other, core)

    def remote(src, dst, send, recv, to):
        return pltpu.make_async_remote_copy(
            src_ref=src, dst_ref=dst, send_sem=send, recv_sem=recv, device_id=to, device_id_type=MESH
        )

    barrier = pltpu.get_barrier_semaphore()

    def greet(to):
        pl.semaphore_signal(barrier, inc=1, device_id=to, device_id_type=MESH)

    @pl.when(active)
    def _():
        loop(1, 16, lambda d: greet(peer_z(lax.rem(z + d, 16))))
        loop(1, 4, lambda d: greet(peer_x(lax.rem(x + d, 4))))
        loop(1, 8, lambda d: greet(peer_yc(lax.rem(me + d, 8))))
        pl.semaphore_wait(barrier, 25)

    @pl.when(jnp.logical_not(active))
    def _():
        loop(0, 8, lambda h: greet(peer_z(h * 2)))
        pl.semaphore_wait(barrier, 8)

    def rows_of(group):
        return pl.ds(0, 4) if group < 2 else pl.ds((group - 2) * PER, PER)

    def of(group, key, value, query):
        return (key, value)[group] if group < 2 else query

    def in_copy(group, head):
        rows = rows_of(group)
        src = of(group, k_in, v_in, q_in).at[rows, :, pl.ds(pl.multiple_of(head * 128, 128), 128)]
        dst = in_slot(group, z)
        return remote(src, dst, in_send.at[group, head], in_recv.at[group, z], peer_z(head * 2))

    def in_slot(group, source):
        columns = pl.ds(pl.multiple_of(lax.div(source, 4) * 64, 64), 64)
        return of(group, home_k, home_v, home_q).at[lax.rem(source, 4), rows_of(group), columns, :]

    def in_own(group):
        src = of(group, k_in, v_in, q_in).at[rows_of(group), :, pl.ds(pl.multiple_of(near * 128, 128), 128)]
        return pltpu.make_async_copy(src, in_slot(group, z), in_recv.at[group, z])

    def in_start(group):
        @pl.when(active)
        def _():
            in_own(group).start()

        @pl.when(jnp.logical_not(active))
        def _():
            in_copy(group, near).start()

        loop(1, 8, lambda d: in_copy(group, lax.rem(near + d, 8)).start())

    def in_sent(group):
        @pl.when(jnp.logical_not(active))
        def _():
            in_copy(group, near).wait_send()

        loop(1, 8, lambda d: in_copy(group, lax.rem(near + d, 8)).wait_send())

    def in_wait(group):
        in_own(group).wait()

        def one(d):
            source = lax.rem(z + d, 16)
            slot = in_slot(group, source)
            remote(slot, slot, in_send.at[group, 0], in_recv.at[group, source], peer_z(source)).wait_recv()

        loop(1, 16, one)

    def row_slot(group, source):
        columns = pl.ds(pl.multiple_of(source * 256, 256), 256)
        return of(group, row_k, row_v, row_q).at[rows_of(group), columns, :]

    def row_copy(group, other):
        src = of(group, home_k, home_v, home_q).at[other, rows_of(group)]
        return remote(src, row_slot(group, x), row_send.at[group, other], row_recv.at[group, x], peer_x(other))

    def row_own(group):
        src = of(group, home_k, home_v, home_q).at[x, rows_of(group)]
        return pltpu.make_async_copy(src, row_slot(group, x), row_recv.at[group, x])

    def row_wait(group):
        row_own(group).wait()

        def one(d):
            source = lax.rem(x + d, 4)
            slot = row_slot(group, source)
            remote(slot, slot, row_send.at[group, source], row_recv.at[group, source], peer_x(source)).wait_recv()

        loop(1, 4, one)

    def col_slot(group, source):
        of_y, of_core = lax.div(source, 2), lax.rem(source, 2)
        if group < 2:
            return (col_k, col_v)[group].at[of_y, :, of_core]
        return col_q.at[group - 2, of_y, :, of_core]

    def col_source(group, other):
        columns = pl.ds(pl.multiple_of(other * 32, 32), 32)
        return of(group, home_k, home_v, home_q).at[:, rows_of(group), columns, :]

    def col_copy(group, other):
        return remote(
            col_source(group, other),
            col_slot(group, me),
            col_send.at[group, other],
            col_recv.at[group, me],
            peer_yc(other),
        )

    def col_own(group):
        return pltpu.make_async_copy(col_source(group, me), col_slot(group, me), col_recv.at[group, me])

    def col_wait(group):
        col_own(group).wait()

        def one(d):
            source = lax.rem(me + d, 8)
            slot = col_slot(group, source)
            remote(slot, slot, col_send.at[group, source], col_recv.at[group, source], peer_yc(source)).wait_recv()

        loop(1, 8, one)

    def spread(group):
        row_own(group).start()
        col_own(group).start()
        loop(1, 4, lambda d: row_copy(group, lax.rem(x + d, 4)).start())
        loop(1, 8, lambda d: col_copy(group, lax.rem(me + d, 8)).start())

    def spread_sent(group):
        loop(1, 4, lambda d: row_copy(group, lax.rem(x + d, 4)).wait_send())
        loop(1, 8, lambda d: col_copy(group, lax.rem(me + d, 8)).wait_send())

    def row_back(batch, other, source, target):
        rows = pl.ds(batch * PER, PER)
        columns = pl.ds(pl.multiple_of(target * 256, 256), 256)
        part = remote(
            row_part.at[rows, columns, :],
            home_row_part.at[source, rows],
            row_back_send.at[batch, 0, other],
            row_back_recv.at[batch, 0, source],
            peer_x(other),
        )
        level = remote(
            row_level.at[batch, columns, :],
            home_row_level.at[batch, source],
            row_back_send.at[batch, 1, other],
            row_back_recv.at[batch, 1, source],
            peer_x(other),
        )
        return part, level

    def row_back_own(batch):
        rows = pl.ds(batch * PER, PER)
        columns = pl.ds(pl.multiple_of(x * 256, 256), 256)
        return (
            pltpu.make_async_copy(
                row_part.at[rows, columns, :], home_row_part.at[x, rows], row_back_recv.at[batch, 0, x]
            ),
            pltpu.make_async_copy(
                row_level.at[batch, columns, :], home_row_level.at[batch, x], row_back_recv.at[batch, 1, x]
            ),
        )

    def col_back(batch, other, source, target):
        rows = pl.ds(batch * PER, PER)
        columns = pl.ds(pl.multiple_of(source * 32, 32), 32)
        part = remote(
            col_part.at[batch, lax.div(target, 2), :, lax.rem(target, 2)],
            home_col_part.at[:, rows, columns, :],
            col_back_send.at[batch, 0, other],
            col_back_recv.at[batch, 0, source],
            peer_yc(other),
        )
        level = remote(
            col_level.at[batch],
            home_col_level.at[batch, columns, :],
            col_back_send.at[batch, 1, other],
            col_back_recv.at[batch, 1, source],
            peer_yc(other),
        )
        return part, level

    def col_back_own(batch):
        rows = pl.ds(batch * PER, PER)
        columns = pl.ds(pl.multiple_of(me * 32, 32), 32)
        return (
            pltpu.make_async_copy(
                col_part.at[batch, y, :, core],
                home_col_part.at[:, rows, columns, :],
                col_back_recv.at[batch, 0, me],
            ),
            pltpu.make_async_copy(
                col_level.at[batch], home_col_level.at[batch, columns, :], col_back_recv.at[batch, 1, me]
            ),
        )

    def start_both(pair):
        for copy in pair:
            copy.start()

    def row_return(batch):
        start_both(row_back_own(batch))

        def one(d):
            other = lax.rem(x + d, 4)
            start_both(row_back(batch, other, x, other))

        loop(1, 4, one)

    def col_return(batch):
        start_both(col_back_own(batch))

        def one(d):
            other = lax.rem(me + d, 8)
            start_both(col_back(batch, other, me, other))

        loop(1, 8, one)

    def return_wait(batch):
        for copy in row_back_own(batch) + col_back_own(batch):
            copy.wait()

        def one_row(d):
            other = lax.rem(x + d, 4)
            for copy in row_back(batch, other, other, x):
                copy.wait_recv()

        def one_col(d):
            other = lax.rem(me + d, 8)
            for copy in col_back(batch, other, other, me):
                copy.wait_recv()

        loop(1, 4, one_row)
        loop(1, 8, one_col)

    def return_sent(batch):
        def one_row(d):
            other = lax.rem(x + d, 4)
            for copy in row_back(batch, other, x, other):
                copy.wait_send()

        def one_col(d):
            other = lax.rem(me + d, 8)
            for copy in col_back(batch, other, me, other):
                copy.wait_send()

        loop(1, 4, one_row)
        loop(1, 8, one_col)

    def out_slot(batch, head):
        return out.at[pl.ds(batch * PER, PER), :, pl.ds(pl.multiple_of(head * 128, 128), 128)]

    def out_source(batch, other):
        columns = pl.ds(pl.multiple_of(lax.div(other, 4) * 64, 64), 64)
        return home_context.at[lax.rem(other, 4), pl.ds(batch * PER, PER), columns, :]

    def out_copy(batch, other):
        return remote(
            out_source(batch, other),
            out_slot(batch, near),
            out_send.at[batch, other],
            out_recv.at[batch, near],
            peer_z(other),
        )

    def out_own(batch):
        return pltpu.make_async_copy(out_source(batch, z), out_slot(batch, near), out_recv.at[batch, near])

    def out_start(batch):
        out_own(batch).start()
        loop(1, 16, lambda d: out_copy(batch, lax.rem(z + d, 16)).start())

    def out_sent(batch):
        loop(1, 16, lambda d: out_copy(batch, lax.rem(z + d, 16)).wait_send())

    def out_arrived(batch):
        def one(head):
            slot = out_slot(batch, head)
            remote(slot, slot, out_send.at[batch, 0], out_recv.at[batch, head], peer_z(head * 2)).wait_recv()

        @pl.when(active)
        def _():
            out_own(batch).wait()

        @pl.when(jnp.logical_not(active))
        def _():
            one(near)

        loop(1, 8, lambda d: one(lax.rem(near + d, 8)))

    def row_work(batch):
        row_level[batch] = jnp.zeros((1024, 128), jnp.bfloat16)
        lane = lax.broadcasted_iota(jnp.int32, (BLOCK, 128), 1)
        causal = lax.broadcasted_iota(jnp.int32, (BLOCK, BLOCK), 0) >= lax.broadcasted_iota(
            jnp.int32, (BLOCK, BLOCK), 1
        )

        def one(step):
            r = batch * PER + step
            mark = (y * 8 + x * 2 + core) * PER + step
            for at in range(1024 // BLOCK):
                here = pl.ds(at * BLOCK, BLOCK)
                query = row_q[r, here]
                scores = lax.dot_general(
                    query, row_k[r, pl.ds(0, (at + 1) * BLOCK)], NT, preferred_element_type=jnp.float32
                )
                last = jnp.where(causal, scores[:, at * BLOCK :], MASKED)
                scores = jnp.concatenate([scores[:, : at * BLOCK], last], axis=1) if at else last
                best = jnp.max(scores, axis=1, keepdims=True)
                weights = jnp.exp((scores - best) * SCALE)
                total = jnp.maximum(jnp.sum(weights, axis=1, keepdims=True), 1.0)
                summed = jnp.dot(
                    weights.astype(jnp.bfloat16),
                    row_v[r, pl.ds(0, (at + 1) * BLOCK)],
                    preferred_element_type=jnp.float32,
                )
                row_part[r, here] = (summed / total).astype(jnp.bfloat16)
                level = (best * SCALE + jnp.log(total)).astype(jnp.bfloat16).astype(jnp.float32)
                old = row_level[batch, here].astype(jnp.float32)
                row_level[batch, here] = jnp.where(lane == mark, level, old).astype(jnp.bfloat16)

        loop(0, PER, one)

    def widen(target, source, rows):
        def one(block):
            of_y, of_z, of_core = lax.div(block, 8), lax.rem(lax.div(block, 2), 4), lax.rem(block, 2)
            piece = source[of_y, of_z, of_core].astype(jnp.float32).reshape(rows * 32, 128)
            target[pl.ds(pl.multiple_of(block * rows * 32, 32), rows * 32)] = piece

        loop(0, 32, one)

    def col_work(batch):
        queries = 32 * PER
        widen(wide_q, col_q.at[batch], PER)
        at = lax.broadcasted_iota(jnp.int32, (queries, 128), 0)
        lane = lax.broadcasted_iota(jnp.int32, (queries, 128), 1)
        lower = lax.div(at, PER) * 4 + batch * PER + lax.rem(at, PER) > lane

        def one(c, levels):
            query = wide_q[pl.ds(c, queries, stride=32), :].astype(jnp.bfloat16)
            key = wide_k[pl.ds(c, 128, stride=32), :].astype(jnp.bfloat16)
            value = wide_v[pl.ds(c, 128, stride=32), :].astype(jnp.bfloat16)
            scores = lax.dot_general(query, key, NT, preferred_element_type=jnp.float32) * SCALE
            best = jnp.max(jnp.where(lower, scores, MASKED), axis=1, keepdims=True)
            weights = jnp.where(lower, jnp.exp(scores - best), 0.0)
            total = jnp.maximum(jnp.sum(weights, axis=1, keepdims=True), 1.0)
            summed = jnp.dot(weights.astype(jnp.bfloat16), value, preferred_element_type=jnp.float32)
            wide_o[pl.ds(c, queries, stride=32), :] = summed / total
            return jnp.where(lane == c, best + jnp.log(total), levels)

        levels = lax.fori_loop(0, 32, one, jnp.zeros((queries, 128), jnp.float32), unroll=4)
        levels = jnp.concatenate([levels, jnp.zeros((128 - queries, 128), jnp.float32)], axis=0)
        col_level[batch] = levels.T[:32].astype(jnp.bfloat16)

        def narrow(block):
            of_y, of_z, of_core = lax.div(block, 8), lax.rem(lax.div(block, 2), 4), lax.rem(block, 2)
            piece = wide_o[pl.ds(pl.multiple_of(block * PER * 32, 32), PER * 32)]
            col_part[batch, of_y, of_z, of_core] = piece.astype(jnp.bfloat16).reshape(PER, 32, 128)

        loop(0, 32, narrow)

    def combine(batch):
        row_levels = home_row_level[batch, 0].astype(jnp.float32)
        for source in range(1, 4):
            row_levels = row_levels + home_row_level[batch, source].astype(jnp.float32)
        col_levels = home_col_level[batch].astype(jnp.float32)
        top = jnp.maximum(row_levels, col_levels)
        row_factor = jnp.exp(row_levels - top)
        col_factor = jnp.exp(col_levels - top)
        denom = row_factor + col_factor
        shift = lax.rem(128 - (y * 8 + core) * PER, 128)
        row_factor = pltpu.roll(row_factor / denom, shift, 1)
        col_factor = pltpu.roll(col_factor / denom, shift, 1)
        for source in range(4):
            for step in range(PER):
                lane = source * 2 * PER + step
                r = batch * PER + step
                home_context[source, r] = (
                    row_factor[:, lane : lane + 1] * home_row_part[source, r].astype(jnp.float32)
                    + col_factor[:, lane : lane + 1] * home_col_part[source, r].astype(jnp.float32)
                ).astype(jnp.bfloat16)

    in_start(0)
    in_start(1)
    for batch in range(BATCHES):
        if batch < 2:
            in_sent(batch)
        in_start(2 + batch)

        if batch < 2:

            @pl.when(active)
            def _(batch=batch):
                in_wait(batch)
                spread(batch)

    @pl.when(active)
    def _():
        for batch in range(BATCHES):
            in_wait(2 + batch)
            spread(2 + batch)
            if batch > 0:
                return_wait(batch - 1)
                combine(batch - 1)
                out_start(batch - 1)
            if batch == 0:
                row_wait(0)
                row_wait(1)
            row_wait(2 + batch)
            row_work(batch)
            row_return(batch)
            if batch == 0:
                col_wait(0)
                widen(wide_k, col_k, 4)
                col_wait(1)
                widen(wide_v, col_v, 4)
            col_wait(2 + batch)
            col_work(batch)
            col_return(batch)
        return_wait(BATCHES - 1)
        combine(BATCHES - 1)
        out_start(BATCHES - 1)
        for group in range(GROUPS):
            spread_sent(group)
        for batch in range(BATCHES):
            return_sent(batch)
            out_sent(batch)

    for batch in range(BATCHES):
        in_sent(2 + batch)
    for batch in range(BATCHES):
        out_arrived(batch)


def attention(queries, key_vectors, values):
    bf16, f32 = jnp.bfloat16, jnp.float32
    dma = pltpu.SemaphoreType.DMA
    home = pltpu.VMEM((4, 4, 256, 128), bf16)
    rows = pltpu.VMEM((4, 1024, 128), bf16)
    batches = pltpu.VMEM((BATCHES, 4, 4, 2, PER, 32, 128), bf16)
    columns = pltpu.VMEM((4, 4, 2, 4, 32, 128), bf16)
    anywhere = pl.BlockSpec(memory_space=pl.ANY)
    return pl.pallas_call(
        kernel,
        out_shape=jax.ShapeDtypeStruct(queries.shape, bf16),
        in_specs=[anywhere] * 3,
        out_specs=anywhere,
        scratch_shapes=[
            home,
            home,
            home,
            rows,
            rows,
            rows,
            batches,
            columns,
            columns,
            rows,
            pltpu.VMEM((BATCHES, 1024, 128), bf16),
            batches,
            pltpu.VMEM((BATCHES, 32, 128), bf16),
            home,
            pltpu.VMEM((BATCHES, 4, 256, 128), bf16),
            home,
            pltpu.VMEM((BATCHES, 256, 128), bf16),
            home,
            pltpu.VMEM((32 * PER * 32, 128), f32),
            pltpu.VMEM((4096, 128), f32),
            pltpu.VMEM((4096, 128), f32),
            pltpu.VMEM((32 * PER * 32, 128), f32),
            dma((GROUPS, 8)),
            dma((GROUPS, 16)),
            dma((GROUPS, 4)),
            dma((GROUPS, 4)),
            dma((GROUPS, 8)),
            dma((GROUPS, 8)),
            dma((BATCHES, 2, 4)),
            dma((BATCHES, 2, 4)),
            dma((BATCHES, 2, 8)),
            dma((BATCHES, 2, 8)),
            dma((BATCHES, 16)),
            dma((BATCHES, 8)),
        ],
        compiler_params=pltpu.CompilerParams(
            collective_id=0, has_side_effects=True, vmem_limit_bytes=48 * 1024 * 1024
        ),
    )(queries, key_vectors, values)


def body(queries, key_vectors, values, out_weight):
    rows_dev, cols_dev, width = queries.shape
    context = attention(queries, key_vectors, values)
    flat = context.reshape(rows_dev * cols_dev, width)
    attended = jnp.dot(flat, out_weight, preferred_element_type=jnp.float32).astype(jnp.bfloat16)
    return attended.reshape(rows_dev, cols_dev, width)


def solution(mesh):
    in_specs = (P("row", "col", None), P("row", "col", None), P("row", "col", None), P())
    out_specs = P("row", "col", None)
    return jax.shard_map(body, mesh=mesh, in_specs=in_specs, out_specs=out_specs, check_vma=False)
```

```python
import jax
import jax.numpy as jnp
from jax import lax
from jax.experimental import pallas as pl
from jax.experimental.pallas import tpu as pltpu
from jax.sharding import PartitionSpec as P

HEADS = 8
HEAD_DIM = 128
SCALE = HEAD_DIM**-0.5
BATCHES = 4
PER = 4 // BATCHES
GROUPS = 2 + BATCHES
BLOCK = 256
MASKED = -1e30
MESH = pl.DeviceIdType.MESH
NT = (((1,), (1,)), ((), ()))


def device(x, y, z, core):
    return (y * 8 + lax.rem(z, 4) * 2 + core, x * 4 + lax.div(z, 4))


NEAREST = (0, 1, 7, 2, 6, 3, 5, 4)


def loop(first, last, step, unroll=1):
    def run(i, carry):
        step(i)
        return carry

    lax.fori_loop(first, last, run, 0, unroll=unroll)


def widen(source, target, per):
    def one(block):
        of_z, of_me = lax.div(block, 8), lax.rem(block, 8)
        piece = source[lax.div(of_me, 2), of_z, lax.rem(of_me, 2)]
        target[pl.ds(pl.multiple_of(block * per * 32, 32), per * 32)] = piece.astype(jnp.float32).reshape(
            per * 32, 128
        )

    loop(0, 32, one, 4)


def by_column(source, wide, target):
    widen(source, wide, 4)

    def one(c):
        target[c] = wide[pl.ds(c, 128, stride=32), :].astype(jnp.bfloat16)

    loop(0, 32, one, 8)


def row_item(query_ref, key_ref, value_ref, part_ref, level_ref, step):
    causal = lax.broadcasted_iota(jnp.int32, (BLOCK, BLOCK), 0) >= lax.broadcasted_iota(
        jnp.int32, (BLOCK, BLOCK), 1
    )
    first = (lax.broadcasted_iota(jnp.int32, (16, 128), 1) == 0).astype(jnp.bfloat16)
    for at in range(1024 // BLOCK):
        here, upto = pl.ds(at * BLOCK, BLOCK), pl.ds(0, (at + 1) * BLOCK)
        scores = lax.dot_general(query_ref[here], key_ref[upto], NT, preferred_element_type=jnp.float32)
        last = jnp.where(causal, scores[:, at * BLOCK :], MASKED)
        scores = jnp.concatenate([scores[:, : at * BLOCK], last], axis=1) if at else last
        best = jnp.max(scores, axis=1, keepdims=True)
        weights = jnp.exp((scores - best) * SCALE)
        total = jnp.maximum(jnp.sum(weights, axis=1, keepdims=True), 1.0)
        summed = jnp.dot(weights.astype(jnp.bfloat16), value_ref[upto], preferred_element_type=jnp.float32)
        part_ref[here] = (summed * (1.0 / total)).astype(jnp.bfloat16)
        level = jnp.broadcast_to(best * SCALE + jnp.log(total), (BLOCK, 128)).astype(jnp.bfloat16)
        turned = lax.dot_general(first, level, NT, preferred_element_type=jnp.float32)
        level_ref[step:, here] = turned[: level_ref.shape[0] - step]


def col_scores(query_ref, wide, key_by_col, scores, per):
    widen(query_ref, wide, per)

    def one(c):
        query = wide[pl.ds(c, 32 * per, stride=32), :].astype(jnp.bfloat16)
        scores[c] = lax.dot_general(query, key_by_col[c], NT, preferred_element_type=jnp.float32)

    loop(0, 32, one, 8)


def col_weights(scores, weights, inverse, level_ref, batch, per):
    queries = 32 * per
    at = lax.broadcasted_iota(jnp.int32, (queries, 128), 0)
    lane = lax.broadcasted_iota(jnp.int32, (queries, 128), 1)

    def grid_row(block, r):
        return lax.div(lax.rem(block, 8), 2) * 32 + lax.div(block, 8) * 8 + lax.rem(block, 2) * 4 + r

    lower = grid_row(lax.div(at, per), batch * per + lax.rem(at, per)) > grid_row(lax.div(lane, 4), lax.rem(lane, 4))

    def one(c, levels):
        masked = jnp.where(lower, scores[c], MASKED)
        best = jnp.max(masked, axis=1, keepdims=True)
        weight = jnp.where(lower, jnp.exp((masked - best) * SCALE), 0.0)
        total = jnp.maximum(jnp.sum(weight, axis=1, keepdims=True), 1.0)
        weights[c] = weight.astype(jnp.bfloat16)
        inverse[c] = jnp.broadcast_to(1.0 / total, (queries, 128))
        return jnp.where(lane == c, best * SCALE + jnp.log(total), levels)

    levels = lax.fori_loop(0, 32, one, jnp.zeros((queries, 128), jnp.float32), unroll=8)
    if queries < 128:
        levels = jnp.concatenate([levels, jnp.zeros((128 - queries, 128), jnp.float32)], axis=0)
    level_ref[...] = levels.T[:32].astype(jnp.bfloat16)


def col_sums(weights, inverse, value_by_col, wide, part_ref, per):
    def one(c):
        summed = jnp.dot(weights[c], value_by_col[c], preferred_element_type=jnp.float32)
        wide[pl.ds(c, 32 * per, stride=32), :] = summed * inverse[c]

    loop(0, 32, one, 8)

    def narrow(block):
        of_z, of_me = lax.div(block, 8), lax.rem(block, 8)
        piece = wide[pl.ds(pl.multiple_of(block * per * 32, 32), per * 32)]
        part_ref[lax.div(of_me, 2), of_z, lax.rem(of_me, 2)] = piece.astype(jnp.bfloat16).reshape(per, 32, 128)

    loop(0, 32, narrow, 4)


def combine(row_levels, row_parts, col_levels, col_parts, contexts, batch, shift, per):
    stacked = jnp.concatenate([row_levels[source] for source in range(4)], axis=0)
    if 32 * per < 128:
        stacked = jnp.concatenate([stacked, jnp.zeros((128 - 32 * per, 256), jnp.float32)], axis=0)
    row_level = stacked.T
    col_level = pltpu.roll(col_levels[...].astype(jnp.float32), shift, 1)
    top = jnp.maximum(row_level, col_level)
    row_factor = jnp.exp(row_level - top)
    col_factor = jnp.exp(col_level - top)
    inverse = 1.0 / (row_factor + col_factor)
    row_factor, col_factor = row_factor * inverse, col_factor * inverse
    for source in range(4):
        for step in range(per):
            lane = source * 8 * per + step
            r = batch * per + step
            contexts[source, r] = (
                row_factor[:, lane : lane + 1] * row_parts[source, r].astype(jnp.float32)
                + col_factor[:, lane : lane + 1] * col_parts[source, r].astype(jnp.float32)
            ).astype(jnp.bfloat16)


def kernel(
    q_in,
    k_in,
    v_in,
    out,
    home_q,
    home_k,
    home_v,
    row_q,
    row_k,
    row_v,
    col_q,
    col_k,
    col_v,
    row_part,
    row_level,
    col_part,
    col_level,
    home_row_part,
    home_row_level,
    home_col_part,
    home_col_level,
    home_context,
    key_by_col,
    value_by_col,
    wide,
    wide_q,
    wide_o,
    scores,
    weights,
    inverse,
    in_send,
    in_recv,
    row_send,
    row_recv,
    col_send,
    col_recv,
    row_back_send,
    row_back_recv,
    col_back_send,
    col_back_recv,
    out_send,
    out_recv,
):
    at_row, at_col = lax.axis_index("row"), lax.axis_index("col")
    y, z_lo, core = lax.div(at_row, 8), lax.rem(lax.div(at_row, 2), 4), lax.rem(at_row, 2)
    x, z_hi = lax.div(at_col, 4), lax.rem(at_col, 4)
    z = z_hi * 4 + z_lo
    near = lax.div(z, 2)
    active = lax.rem(z, 2) == 0
    me = y * 2 + core

    def peer_x(other):
        return device(other, y, z, core)

    def peer_yc(other):
        return device(x, lax.div(other, 2), z, lax.rem(other, 2))

    def peer_z(other):
        return device(x, y, other, core)

    def remote(src, dst, send, recv, to):
        return pltpu.make_async_remote_copy(
            src_ref=src, dst_ref=dst, send_sem=send, recv_sem=recv, device_id=to, device_id_type=MESH
        )

    def await_bytes(ref, semaphore):
        pltpu.make_async_copy(ref, ref, semaphore).wait()

    def others(mine, count, step):
        for offset in range(1, count):
            step(lax.rem(mine + offset, count))

    barrier = pltpu.get_barrier_semaphore()

    def greet(to):
        pl.semaphore_signal(barrier, inc=1, device_id=to, device_id_type=MESH)

    @pl.when(active)
    def _():
        others(z, 16, lambda other: greet(peer_z(other)))
        others(x, 4, lambda other: greet(peer_x(other)))
        others(me, 8, lambda other: greet(peer_yc(other)))
        pl.semaphore_wait(barrier, 25)

    @pl.when(jnp.logical_not(active))
    def _():
        for head in range(HEADS):
            greet(peer_z(head * 2))
        pl.semaphore_wait(barrier, 8)

    def rows_of(group):
        return pl.ds(0, 4) if group < 2 else pl.ds((group - 2) * PER, PER)

    def of(group, key, value, query):
        return (key, value)[group] if group < 2 else query

    def in_copy(group, head):
        rows = rows_of(group)
        src = of(group, k_in, v_in, q_in).at[rows, :, pl.ds(pl.multiple_of(head * 128, 128), 128)]
        dst = in_slot(group, z)
        return remote(src, dst, in_send.at[group, head], in_recv.at[group], peer_z(head * 2))

    def in_slot(group, source):
        columns = pl.ds(pl.multiple_of(lax.div(source, 4) * 64, 64), 64)
        return of(group, home_k, home_v, home_q).at[lax.rem(source, 4), rows_of(group), columns, :]

    def in_own(group):
        src = of(group, k_in, v_in, q_in).at[rows_of(group), :, pl.ds(pl.multiple_of(near * 128, 128), 128)]
        return pltpu.make_async_copy(src, in_slot(group, z), in_recv.at[group])

    def in_step(group, offset, before):
        head = lax.rem(near + offset, 8)

        def go():
            if before is not None:
                in_copy(before, head).wait_send()
            if group is not None:
                in_copy(group, head).start()

        if offset:
            go()
        else:

            @pl.when(active)
            def _():
                if group is not None:
                    in_own(group).start()

            @pl.when(jnp.logical_not(active))
            def _():
                go()

    def in_start(group):
        for offset in reversed(NEAREST):
            in_step(group, offset, None)

    def in_next(group):
        for offset in NEAREST:
            in_step(group + 1, offset, group)

    def in_sent(group):
        for offset in NEAREST:
            in_step(None, offset, group)

    def in_wait(group):
        await_bytes(of(group, home_k, home_v, home_q).at[:, rows_of(group)], in_recv.at[group])

    def row_slot(group, source):
        columns = pl.ds(pl.multiple_of(source * 256, 256), 256)
        return of(group, row_k, row_v, row_q).at[rows_of(group), columns, :]

    def row_copy(group, other):
        src = of(group, home_k, home_v, home_q).at[other, rows_of(group)]
        return remote(src, row_slot(group, x), row_send.at[group], row_recv.at[group], peer_x(other))

    def row_own(group):
        src = of(group, home_k, home_v, home_q).at[x, rows_of(group)]
        return pltpu.make_async_copy(src, row_slot(group, x), row_recv.at[group])

    def row_wait(group):
        await_bytes(of(group, row_k, row_v, row_q).at[rows_of(group)], row_recv.at[group])

    def col_slot(group, source):
        of_y, of_core = lax.div(source, 2), lax.rem(source, 2)
        if group < 2:
            return (col_k, col_v)[group].at[of_y, :, of_core]
        return col_q.at[group - 2, of_y, :, of_core]

    def col_source(group, other):
        columns = pl.ds(pl.multiple_of(other * 32, 32), 32)
        return of(group, home_k, home_v, home_q).at[:, rows_of(group), columns, :]

    def col_copy(group, other):
        return remote(
            col_source(group, other), col_slot(group, me), col_send.at[group], col_recv.at[group], peer_yc(other)
        )

    def col_own(group):
        return pltpu.make_async_copy(col_source(group, me), col_slot(group, me), col_recv.at[group])

    def col_wait(group):
        await_bytes((col_k, col_v)[group] if group < 2 else col_q.at[group - 2], col_recv.at[group])

    def spread(group):
        others(x, 4, lambda other: row_copy(group, other).start())
        others(me, 8, lambda other: col_copy(group, other).start())
        row_own(group).start()
        col_own(group).start()

    def spread_sent(group):
        home = of(group, home_k, home_v, home_q)
        await_bytes(home.at[pl.ds(0, 3), rows_of(group)], row_send.at[group])
        await_bytes(home.at[:, rows_of(group), pl.ds(0, 224), :], col_send.at[group])

    def row_back(batch, other, copy):
        rows = pl.ds(batch * PER, PER)
        columns = pl.ds(pl.multiple_of(other * 256, 256), 256)
        copy(
            row_part.at[rows, columns, :],
            home_row_part.at[x, rows],
            row_back_send.at[batch, 0],
            row_back_recv.at[batch, 0],
        )
        copy(
            row_level.at[batch, :, columns],
            home_row_level.at[batch, x],
            row_back_send.at[batch, 1],
            row_back_recv.at[batch, 1],
        )

    def col_back(batch, other, copy):
        columns = pl.ds(pl.multiple_of(me * 32, 32), 32)
        copy(
            col_part.at[batch, lax.div(other, 2), :, lax.rem(other, 2)],
            home_col_part.at[:, pl.ds(batch * PER, PER), columns, :],
            col_back_send.at[batch, 0],
            col_back_recv.at[batch, 0],
        )
        copy(
            col_level.at[batch],
            home_col_level.at[batch, columns, :],
            col_back_send.at[batch, 1],
            col_back_recv.at[batch, 1],
        )

    def send_to(device_id):
        return lambda src, dst, send, recv: remote(src, dst, send, recv, device_id).start()

    def keep(src, dst, send, recv):
        pltpu.make_async_copy(src, dst, recv).start()

    def row_return(batch):
        others(x, 4, lambda other: row_back(batch, other, send_to(peer_x(other))))
        row_back(batch, x, keep)

    def col_return(batch):
        others(me, 8, lambda other: col_back(batch, other, send_to(peer_yc(other))))
        col_back(batch, me, keep)

    def return_wait(batch):
        rows = pl.ds(batch * PER, PER)
        await_bytes(home_row_part.at[:, rows], row_back_recv.at[batch, 0])
        await_bytes(home_row_level.at[batch], row_back_recv.at[batch, 1])
        await_bytes(home_col_part.at[:, rows], col_back_recv.at[batch, 0])
        await_bytes(home_col_level.at[batch], col_back_recv.at[batch, 1])

    def return_sent(batch):
        rows = pl.ds(batch * PER, PER)
        await_bytes(row_part.at[rows, pl.ds(0, 768), :], row_back_send.at[batch, 0])
        await_bytes(row_level.at[batch, :, pl.ds(0, 768)], row_back_send.at[batch, 1])
        await_bytes(home_col_part.at[:, rows, pl.ds(0, 224), :], col_back_send.at[batch, 0])
        await_bytes(home_col_level.at[batch, pl.ds(0, 224), :], col_back_send.at[batch, 1])

    def out_slot(batch, head):
        return out.at[pl.ds(batch * PER, PER), :, pl.ds(pl.multiple_of(head * 128, 128), 128)]

    def out_source(batch, other):
        columns = pl.ds(pl.multiple_of(lax.div(other, 4) * 64, 64), 64)
        return home_context.at[lax.rem(other, 4), pl.ds(batch * PER, PER), columns, :]

    def out_copy(batch, other):
        return remote(
            out_source(batch, other), out_slot(batch, near), out_send.at[batch], out_recv.at[batch], peer_z(other)
        )

    def out_start(batch):
        others(z, 16, lambda other: out_copy(batch, other).start())
        pltpu.make_async_copy(out_source(batch, z), out_slot(batch, near), out_recv.at[batch]).start()

    def out_sent(batch):
        await_bytes(row_part.at[pl.ds(batch * PER, PER), pl.ds(0, 960), :], out_send.at[batch])

    def out_arrived(batch):
        await_bytes(out.at[pl.ds(batch * PER, PER)], out_recv.at[batch])

    def work(batch):
        row_wait(2 + batch)
        for step in range(PER):
            r = batch * PER + step
            row_item(row_q.at[r], row_k.at[r], row_v.at[r], row_part.at[r], row_level.at[batch], step)
        row_return(batch)
        col_wait(2 + batch)
        col_scores(col_q.at[batch], wide_q, key_by_col, scores, PER)
        col_weights(scores, weights, inverse, col_level.at[batch], batch, PER)
        col_sums(weights, inverse, value_by_col, wide_o, col_part.at[batch], PER)
        col_return(batch)

    def finish(batch):
        return_wait(batch)
        combine(
            home_row_level.at[batch],
            home_row_part,
            home_col_level.at[batch],
            home_col_part,
            home_context,
            batch,
            lax.rem(128 - me * PER, 128),
            PER,
        )
        out_start(batch)

    in_start(0)
    for group in range(2):
        in_next(group)

        @pl.when(active)
        def _(group=group):
            in_wait(group)
            spread(group)
            if group == 0:
                col_wait(0)
                by_column(col_k, wide, key_by_col)

    for batch in range(BATCHES):
        if batch + 1 < BATCHES:
            in_next(2 + batch)

        @pl.when(active)
        def _(batch=batch):
            in_wait(2 + batch)
            spread(2 + batch)
            if batch > 1:
                finish(batch - 2)
            if batch == 1:
                col_wait(1)
                by_column(col_v, wide, value_by_col)
                row_wait(0)
                row_wait(1)
            if batch > 0:
                work(batch - 1)

    @pl.when(active)
    def _():
        work(BATCHES - 1)
        finish(BATCHES - 2)
        finish(BATCHES - 1)
        for group in range(GROUPS):
            spread_sent(group)
        for batch in range(BATCHES):
            return_sent(batch)
            out_sent(batch)

    in_sent(GROUPS - 1)
    for batch in range(BATCHES):
        out_arrived(batch)


def attention(queries, key_vectors, values):
    bf16, f32 = jnp.bfloat16, jnp.float32
    dma = pltpu.SemaphoreType.DMA
    home = pltpu.VMEM((4, 4, 256, 128), bf16)
    rows = pltpu.VMEM((4, 1024, 128), bf16)
    batches = pltpu.VMEM((BATCHES, 4, 4, 2, PER, 32, 128), bf16)
    columns = pltpu.VMEM((4, 4, 2, 4, 32, 128), bf16)
    anywhere = pl.BlockSpec(memory_space=pl.ANY)
    return pl.pallas_call(
        kernel,
        out_shape=jax.ShapeDtypeStruct(queries.shape, bf16),
        in_specs=[anywhere] * 3,
        out_specs=anywhere,
        scratch_shapes=[
            home,
            home,
            home,
            rows,
            rows,
            rows,
            batches,
            columns,
            columns,
            rows,
            pltpu.VMEM((BATCHES, 8 * PER, 1024), f32),
            batches,
            pltpu.VMEM((BATCHES, 32, 128), bf16),
            home,
            pltpu.VMEM((BATCHES, 4, 8 * PER, 256), f32),
            home,
            pltpu.VMEM((BATCHES, 256, 128), bf16),
            home,
            pltpu.VMEM((32, 128, 128), bf16),
            pltpu.VMEM((32, 128, 128), bf16),
            pltpu.VMEM((4096, 128), f32),
            pltpu.VMEM((32 * PER * 32, 128), f32),
            pltpu.VMEM((32 * PER * 32, 128), f32),
            pltpu.VMEM((32, 32 * PER, 128), f32),
            pltpu.VMEM((32, 32 * PER, 128), bf16),
            pltpu.VMEM((32, 32 * PER, 128), f32),
            dma((GROUPS, 8)),
            dma((GROUPS,)),
            dma((GROUPS,)),
            dma((GROUPS,)),
            dma((GROUPS,)),
            dma((GROUPS,)),
            dma((BATCHES, 2)),
            dma((BATCHES, 2)),
            dma((BATCHES, 2)),
            dma((BATCHES, 2)),
            dma((BATCHES,)),
            dma((BATCHES,)),
        ],
        compiler_params=pltpu.CompilerParams(
            collective_id=0, has_side_effects=True, vmem_limit_bytes=60 * 1024 * 1024
        ),
    )(queries, key_vectors, values)


def body(queries, key_vectors, values, out_weight):
    rows_dev, cols_dev, width = queries.shape
    context = attention(queries, key_vectors, values)
    flat = context.reshape(rows_dev * cols_dev, width)
    attended = jnp.dot(flat, out_weight, preferred_element_type=jnp.float32).astype(jnp.bfloat16)
    return attended.reshape(rows_dev, cols_dev, width)


def solution(mesh):
    in_specs = (P("row", "col", None), P("row", "col", None), P("row", "col", None), P())
    out_specs = P("row", "col", None)
    return jax.shard_map(body, mesh=mesh, in_specs=in_specs, out_specs=out_specs, check_vma=False)
```

```python
import jax
import jax.numpy as jnp
from jax import lax
from jax.experimental import pallas as pl
from jax.experimental.pallas import tpu as pltpu
from jax.sharding import PartitionSpec as P

HEADS = 8
HEAD_DIM = 128
SCALE = HEAD_DIM**-0.5
BATCHES = 4
PER = 4 // BATCHES
GROUPS = 2 + BATCHES
BLOCK = 256
MASKED = -1e30
RELAYED = 2
WAY = -4
MESH = pl.DeviceIdType.MESH
NT = (((1,), (1,)), ((), ()))


def device(x, y, z, core):
    return (y * 8 + lax.rem(z, 4) * 2 + core, x * 4 + lax.div(z, 4))


NEAREST = (0, 1, 7, 2, 6, 3, 5, 4)


def loop(first, last, step, unroll=1):
    def run(i, carry):
        step(i)
        return carry

    lax.fori_loop(first, last, run, 0, unroll=unroll)


def widen(source, target, per):
    def one(block):
        of_z, of_me = lax.div(block, 8), lax.rem(block, 8)
        piece = source[lax.div(of_me, 2), of_z, lax.rem(of_me, 2)]
        target[pl.ds(pl.multiple_of(block * per * 32, 32), per * 32)] = piece.astype(jnp.float32).reshape(
            per * 32, 128
        )

    loop(0, 32, one, 4)


def by_column(source, wide, target):
    widen(source, wide, 4)

    def one(c):
        target[c] = wide[pl.ds(c, 128, stride=32), :].astype(jnp.bfloat16)

    loop(0, 32, one, 8)


def row_item(query_ref, key_ref, value_ref, part_ref, level_ref, step):
    causal = lax.broadcasted_iota(jnp.int32, (BLOCK, BLOCK), 0) >= lax.broadcasted_iota(
        jnp.int32, (BLOCK, BLOCK), 1
    )
    first = (lax.broadcasted_iota(jnp.int32, (16, 128), 1) == 0).astype(jnp.bfloat16)
    for at in range(1024 // BLOCK):
        here, upto = pl.ds(at * BLOCK, BLOCK), pl.ds(0, (at + 1) * BLOCK)
        scores = lax.dot_general(query_ref[here], key_ref[upto], NT, preferred_element_type=jnp.float32)
        last = jnp.where(causal, scores[:, at * BLOCK :], MASKED)
        scores = jnp.concatenate([scores[:, : at * BLOCK], last], axis=1) if at else last
        best = jnp.max(scores, axis=1, keepdims=True)
        weights = jnp.exp((scores - best) * SCALE)
        total = jnp.maximum(jnp.sum(weights, axis=1, keepdims=True), 1.0)
        summed = jnp.dot(weights.astype(jnp.bfloat16), value_ref[upto], preferred_element_type=jnp.float32)
        part_ref[here] = (summed * (1.0 / total)).astype(jnp.bfloat16)
        level = jnp.broadcast_to(best * SCALE + jnp.log(total), (BLOCK, 128)).astype(jnp.bfloat16)
        turned = lax.dot_general(first, level, NT, preferred_element_type=jnp.float32)
        level_ref[step:, here] = turned[: level_ref.shape[0] - step]


def col_scores(query_ref, wide, key_by_col, scores, per):
    widen(query_ref, wide, per)

    def one(c):
        query = wide[pl.ds(c, 32 * per, stride=32), :].astype(jnp.bfloat16)
        scores[c] = lax.dot_general(query, key_by_col[c], NT, preferred_element_type=jnp.float32)

    loop(0, 32, one, 8)


def col_weights(scores, weights, inverse, part_ref, batch, per):
    queries = 32 * per
    at = lax.broadcasted_iota(jnp.int32, (queries, 128), 0)
    lane = lax.broadcasted_iota(jnp.int32, (queries, 128), 1)

    def grid_row(block, r):
        return lax.div(lax.rem(block, 8), 2) * 32 + lax.div(block, 8) * 8 + lax.rem(block, 2) * 4 + r

    lower = grid_row(lax.div(at, per), batch * per + lax.rem(at, per)) > grid_row(lax.div(lane, 4), lax.rem(lane, 4))

    def one(c, levels):
        masked = jnp.where(lower, scores[c], MASKED)
        best = jnp.max(masked, axis=1, keepdims=True)
        weight = jnp.where(lower, jnp.exp((masked - best) * SCALE), 0.0)
        total = jnp.maximum(jnp.sum(weight, axis=1, keepdims=True), 1.0)
        weights[c] = weight.astype(jnp.bfloat16)
        inverse[c] = jnp.broadcast_to(1.0 / total, (queries, 128))
        return jnp.where(lane == c, best * SCALE + jnp.log(total), levels)

    levels = lax.fori_loop(0, 32, one, jnp.zeros((queries, 128), jnp.float32), unroll=8)
    if queries < 128:
        levels = jnp.concatenate([levels, jnp.zeros((128 - queries, 128), jnp.float32)], axis=0)
    level = levels.T[:32].astype(jnp.bfloat16)
    for of_me in range(8):
        part_ref[of_me // 2, 4, of_me % 2, 0] = level


def col_sums(weights, inverse, value_by_col, wide, part_ref, per):
    def one(c):
        summed = jnp.dot(weights[c], value_by_col[c], preferred_element_type=jnp.float32)
        wide[pl.ds(c, 32 * per, stride=32), :] = summed * inverse[c]

    loop(0, 32, one, 8)

    def narrow(block):
        of_z, of_me = lax.div(block, 8), lax.rem(block, 8)
        piece = wide[pl.ds(pl.multiple_of(block * per * 32, 32), per * 32)]
        part_ref[lax.div(of_me, 2), of_z, lax.rem(of_me, 2)] = piece.astype(jnp.bfloat16).reshape(per, 32, 128)

    loop(0, 32, narrow, 4)


def combine(row_levels, row_parts, col_levels, col_parts, contexts, batch, shift, per):
    stacked = jnp.concatenate([row_levels[source] for source in range(4)], axis=0)
    if 32 * per < 128:
        stacked = jnp.concatenate([stacked, jnp.zeros((128 - 32 * per, 256), jnp.float32)], axis=0)
    row_level = stacked.T
    col_level = pltpu.roll(col_levels[...].astype(jnp.float32), shift, 1)
    top = jnp.maximum(row_level, col_level)
    row_factor = jnp.exp(row_level - top)
    col_factor = jnp.exp(col_level - top)
    inverse = 1.0 / (row_factor + col_factor)
    row_factor, col_factor = row_factor * inverse, col_factor * inverse
    for source in range(4):
        for step in range(per):
            lane = source * 8 * per + step
            r = batch * per + step
            contexts[source, r] = (
                row_factor[:, lane : lane + 1] * row_parts[source, r].astype(jnp.float32)
                + col_factor[:, lane : lane + 1] * col_parts[source, r].astype(jnp.float32)
            ).astype(jnp.bfloat16)


def kernel(
    q_in,
    k_in,
    v_in,
    out,
    home_q,
    home_k,
    home_v,
    row_q,
    row_k,
    row_v,
    col_q,
    col_k,
    col_v,
    row_part,
    row_level,
    col_part,
    home_row_part,
    home_row_level,
    home_col_part,
    home_context,
    key_by_col,
    value_by_col,
    wide,
    wide_q,
    wide_o,
    scores,
    weights,
    inverse,
    in_send,
    in_recv,
    row_send,
    row_recv,
    col_send,
    col_recv,
    row_back_send,
    row_back_recv,
    col_back_send,
    col_back_recv,
    out_send,
    out_recv,
    relay,
    relay_send,
    relay_recv,
):
    at_row, at_col = lax.axis_index("row"), lax.axis_index("col")
    y, z_lo, core = lax.div(at_row, 8), lax.rem(lax.div(at_row, 2), 4), lax.rem(at_row, 2)
    x, z_hi = lax.div(at_col, 4), lax.rem(at_col, 4)
    z = z_hi * 4 + z_lo
    near = lax.div(z, 2)
    active = lax.rem(z, 2) == 0
    me = y * 2 + core
    relaying = jnp.logical_and(active, core == 1)

    def peer_x(other):
        return device(other, y, z, core)

    def peer_yc(other):
        return device(x, lax.div(other, 2), z, lax.rem(other, 2))

    def peer_z(other):
        return device(x, y, other, core)

    def remote(src, dst, send, recv, to):
        return pltpu.make_async_remote_copy(
            src_ref=src, dst_ref=dst, send_sem=send, recv_sem=recv, device_id=to, device_id_type=MESH
        )

    def await_bytes(ref, semaphore):
        pltpu.make_async_copy(ref, ref, semaphore).wait()

    def others(mine, count, step):
        for offset in range(1, count):
            step(lax.rem(mine + offset, count))

    barrier = pltpu.get_barrier_semaphore()

    def greet(to):
        pl.semaphore_signal(barrier, inc=1, device_id=to, device_id_type=MESH)

    @pl.when(active)
    def _():
        others(z, 16, lambda other: greet(peer_z(other)))
        others(x, 4, lambda other: greet(peer_x(other)))
        others(me, 8, lambda other: greet(peer_yc(other)))
        pl.semaphore_wait(barrier, 25)

    @pl.when(jnp.logical_not(active))
    def _():
        for head in range(HEADS):
            greet(peer_z(head * 2))
        pl.semaphore_wait(barrier, 8)

    def rows_of(group):
        return pl.ds(0, 4) if group < 2 else pl.ds((group - 2) * PER, PER)

    def of(group, key, value, query):
        return (key, value)[group] if group < 2 else query

    def in_copy(group, head):
        rows = rows_of(group)
        src = of(group, k_in, v_in, q_in).at[rows, :, pl.ds(pl.multiple_of(head * 128, 128), 128)]
        dst = in_slot(group, z)
        return remote(src, dst, in_send.at[group, head], in_recv.at[group], peer_z(head * 2))

    def in_slot(group, source):
        columns = pl.ds(pl.multiple_of(lax.div(source, 4) * 64, 64), 64)
        return of(group, home_k, home_v, home_q).at[lax.rem(source, 4), rows_of(group), columns, :]

    def relay_in(group):
        src = (k_in, v_in)[group].at[:, :, pl.ds(pl.multiple_of(lax.rem(near + 4, 8) * 128, 128), 128)]
        return remote(
            src,
            relay.at[group],
            in_send.at[group, lax.rem(near + 4, 8)],
            relay_recv.at[group],
            peer_z(lax.rem(z + 16 + WAY, 16)),
        )

    def relay_on(group):
        return remote(
            relay.at[group],
            in_slot(group, lax.rem(z + 16 - WAY, 16)),
            relay_send.at[group],
            in_recv.at[group],
            peer_z(lax.rem(z + 16 + WAY, 16)),
        )

    def relay_forward(group):
        @pl.when(relaying)
        def _():
            await_bytes(relay.at[group], relay_recv.at[group])
            relay_on(group).start()

    def in_own(group):
        src = of(group, k_in, v_in, q_in).at[rows_of(group), :, pl.ds(pl.multiple_of(near * 128, 128), 128)]
        return pltpu.make_async_copy(src, in_slot(group, z), in_recv.at[group])

    def in_step(group, offset, before):
        head = lax.rem(near + offset, 8)

        def go():
            if before is not None:
                in_copy(before, head).wait_send()
            if group is None:
                return
            if offset == 4 and group < RELAYED:

                @pl.when(relaying)
                def _():
                    relay_in(group).start()

                @pl.when(jnp.logical_not(relaying))
                def _():
                    in_copy(group, head).start()

            else:
                in_copy(group, head).start()

        if offset:
            go()
        else:

            @pl.when(active)
            def _():
                if group is not None:
                    in_own(group).start()

            @pl.when(jnp.logical_not(active))
            def _():
                go()

    def in_start(group):
        for offset in reversed(NEAREST):
            in_step(group, offset, None)

    def in_next(group):
        for offset in NEAREST:
            in_step(group + 1, offset, group)

    def in_sent(group):
        for offset in NEAREST:
            in_step(None, offset, group)

    def in_wait(group):
        await_bytes(of(group, home_k, home_v, home_q).at[:, rows_of(group)], in_recv.at[group])

    def row_slot(group, source):
        columns = pl.ds(pl.multiple_of(source * 256, 256), 256)
        return of(group, row_k, row_v, row_q).at[rows_of(group), columns, :]

    def row_copy(group, other):
        src = of(group, home_k, home_v, home_q).at[other, rows_of(group)]
        return remote(src, row_slot(group, x), row_send.at[group], row_recv.at[group], peer_x(other))

    def row_own(group):
        src = of(group, home_k, home_v, home_q).at[x, rows_of(group)]
        return pltpu.make_async_copy(src, row_slot(group, x), row_recv.at[group])

    def row_wait(group):
        await_bytes(of(group, row_k, row_v, row_q).at[rows_of(group)], row_recv.at[group])

    def col_slot(group, source):
        of_y, of_core = lax.div(source, 2), lax.rem(source, 2)
        if group < 2:
            return (col_k, col_v)[group].at[of_y, :, of_core]
        return col_q.at[group - 2, of_y, :, of_core]

    def col_source(group, other):
        columns = pl.ds(pl.multiple_of(other * 32, 32), 32)
        return of(group, home_k, home_v, home_q).at[:, rows_of(group), columns, :]

    def col_copy(group, other):
        return remote(
            col_source(group, other), col_slot(group, me), col_send.at[group], col_recv.at[group], peer_yc(other)
        )

    def col_own(group):
        return pltpu.make_async_copy(col_source(group, me), col_slot(group, me), col_recv.at[group])

    def col_wait(group):
        await_bytes((col_k, col_v)[group] if group < 2 else col_q.at[group - 2], col_recv.at[group])

    def spread(group):
        others(x, 4, lambda other: row_copy(group, other).start())
        others(me, 8, lambda other: col_copy(group, other).start())
        row_own(group).start()
        col_own(group).start()

    def spread_sent(group):
        home = of(group, home_k, home_v, home_q)
        await_bytes(home.at[pl.ds(0, 3), rows_of(group)], row_send.at[group])
        await_bytes(home.at[:, rows_of(group), pl.ds(0, 224), :], col_send.at[group])

    def row_back(batch, other, copy):
        rows = pl.ds(batch * PER, PER)
        columns = pl.ds(pl.multiple_of(other * 256, 256), 256)
        copy(
            row_part.at[rows, columns, :],
            home_row_part.at[x, rows],
            row_back_send.at[batch, 0],
            row_back_recv.at[batch, 0],
        )
        copy(
            row_level.at[batch, :, columns],
            home_row_level.at[batch, x],
            row_back_send.at[batch, 1],
            row_back_recv.at[batch, 1],
        )

    def col_back(batch, other, copy):
        copy(
            col_part.at[batch, lax.div(other, 2), :, lax.rem(other, 2)],
            home_col_part.at[:, pl.ds(batch * PER, PER), pl.ds(pl.multiple_of(me * 32, 32), 32), :],
            col_back_send.at[batch],
            col_back_recv.at[batch],
        )

    def send_to(device_id):
        return lambda src, dst, send, recv: remote(src, dst, send, recv, device_id).start()

    def keep(src, dst, send, recv):
        pltpu.make_async_copy(src, dst, recv).start()

    def row_return(batch):
        others(x, 4, lambda other: row_back(batch, other, send_to(peer_x(other))))
        row_back(batch, x, keep)

    def col_return(batch):
        others(me, 8, lambda other: col_back(batch, other, send_to(peer_yc(other))))
        col_back(batch, me, keep)

    def return_wait(batch):
        rows = pl.ds(batch * PER, PER)
        await_bytes(home_row_part.at[:, rows], row_back_recv.at[batch, 0])
        await_bytes(home_row_level.at[batch], row_back_recv.at[batch, 1])
        await_bytes(home_col_part.at[:, rows], col_back_recv.at[batch])

    def return_sent(batch):
        rows = pl.ds(batch * PER, PER)
        await_bytes(row_part.at[rows, pl.ds(0, 768), :], row_back_send.at[batch, 0])
        await_bytes(row_level.at[batch, :, pl.ds(0, 768)], row_back_send.at[batch, 1])
        await_bytes(home_col_part.at[:, rows, pl.ds(0, 224), :], col_back_send.at[batch])

    def out_slot(batch, head):
        return out.at[pl.ds(batch * PER, PER), :, pl.ds(pl.multiple_of(head * 128, 128), 128)]

    def out_source(batch, other):
        columns = pl.ds(pl.multiple_of(lax.div(other, 4) * 64, 64), 64)
        return home_context.at[lax.rem(other, 4), pl.ds(batch * PER, PER), columns, :]

    def out_copy(batch, other):
        return remote(
            out_source(batch, other), out_slot(batch, near), out_send.at[batch], out_recv.at[batch], peer_z(other)
        )

    def out_start(batch):
        others(z, 16, lambda other: out_copy(batch, other).start())
        pltpu.make_async_copy(out_source(batch, z), out_slot(batch, near), out_recv.at[batch]).start()

    def out_sent(batch):
        await_bytes(row_part.at[pl.ds(batch * PER, PER), pl.ds(0, 960), :], out_send.at[batch])

    def out_arrived(batch):
        await_bytes(out.at[pl.ds(batch * PER, PER)], out_recv.at[batch])

    def row_work(batch):
        row_wait(2 + batch)
        for step in range(PER):
            r = batch * PER + step
            row_item(row_q.at[r], row_k.at[r], row_v.at[r], row_part.at[r], row_level.at[batch], step)
        row_return(batch)

    def col_work(batch):
        col_wait(2 + batch)
        col_scores(col_q.at[batch], wide_q, key_by_col, scores, PER)
        col_weights(scores, weights, inverse, col_part.at[batch], batch, PER)
        col_sums(weights, inverse, value_by_col, wide_o, col_part.at[batch], PER)
        col_return(batch)

    def finish(batch):
        return_wait(batch)
        combine(
            home_row_level.at[batch],
            home_row_part,
            home_col_part.at[4, batch * PER],
            home_col_part,
            home_context,
            batch,
            lax.rem(128 - me * PER, 128),
            PER,
        )
        out_start(batch)

    in_start(0)
    for group in range(2):
        in_next(group)

        @pl.when(active)
        def _(group=group):
            relay_forward(group)
            in_wait(group)
            spread(group)
            if group == 0:
                col_wait(0)
                by_column(col_k, wide, key_by_col)

    for batch in range(BATCHES):
        if batch + 1 < BATCHES:
            in_next(2 + batch)

        @pl.when(active)
        def _(batch=batch):
            in_wait(2 + batch)
            spread(2 + batch)
            if batch == 3:
                finish(0)
            if batch == 1:
                col_wait(1)
                by_column(col_v, wide, value_by_col)
                row_wait(0)
                row_wait(1)
            if batch > 0:
                row_work(batch - 1)
                col_work(batch - 1)

    @pl.when(active)
    def _():
        finish(1)
        row_work(BATCHES - 1)
        col_work(BATCHES - 1)
        finish(BATCHES - 2)
        finish(BATCHES - 1)
        for group in range(GROUPS):
            spread_sent(group)

        @pl.when(relaying)
        def _():
            for group in range(RELAYED):
                await_bytes(relay.at[group], relay_send.at[group])

        for batch in range(BATCHES):
            return_sent(batch)
            out_sent(batch)

    in_sent(GROUPS - 1)
    for batch in range(BATCHES):
        out_arrived(batch)


def attention(queries, key_vectors, values):
    bf16, f32 = jnp.bfloat16, jnp.float32
    dma = pltpu.SemaphoreType.DMA
    home = pltpu.VMEM((4, 4, 256, 128), bf16)
    rows = pltpu.VMEM((4, 1024, 128), bf16)
    columns = pltpu.VMEM((4, 4, 2, 4, 32, 128), bf16)
    anywhere = pl.BlockSpec(memory_space=pl.ANY)
    return pl.pallas_call(
        kernel,
        out_shape=jax.ShapeDtypeStruct(queries.shape, bf16),
        in_specs=[anywhere] * 3,
        out_specs=anywhere,
        scratch_shapes=[
            home,
            home,
            home,
            rows,
            rows,
            rows,
            pltpu.VMEM((BATCHES, 4, 4, 2, PER, 32, 128), bf16),
            columns,
            columns,
            rows,
            pltpu.VMEM((BATCHES, 8 * PER, 1024), f32),
            pltpu.VMEM((BATCHES, 4, 5, 2, PER, 32, 128), bf16),
            home,
            pltpu.VMEM((BATCHES, 4, 8 * PER, 256), f32),
            pltpu.VMEM((5, 4, 256, 128), bf16),
            home,
            pltpu.VMEM((32, 128, 128), bf16),
            pltpu.VMEM((32, 128, 128), bf16),
            pltpu.VMEM((4096, 128), f32),
            pltpu.VMEM((32 * PER * 32, 128), f32),
            pltpu.VMEM((32 * PER * 32, 128), f32),
            pltpu.VMEM((32, 32 * PER, 128), f32),
            pltpu.VMEM((32, 32 * PER, 128), bf16),
            pltpu.VMEM((32, 32 * PER, 128), f32),
            dma((GROUPS, 8)),
            dma((GROUPS,)),
            dma((GROUPS,)),
            dma((GROUPS,)),
            dma((GROUPS,)),
            dma((GROUPS,)),
            dma((BATCHES, 2)),
            dma((BATCHES, 2)),
            dma((BATCHES,)),
            dma((BATCHES,)),
            dma((BATCHES,)),
            dma((BATCHES,)),
            pltpu.VMEM((RELAYED, 4, 64, 128), bf16),
            dma((RELAYED,)),
            dma((RELAYED,)),
        ],
        compiler_params=pltpu.CompilerParams(
            collective_id=0, has_side_effects=True, vmem_limit_bytes=60 * 1024 * 1024
        ),
    )(queries, key_vectors, values)


def body(queries, key_vectors, values, out_weight):
    rows_dev, cols_dev, width = queries.shape
    context = attention(queries, key_vectors, values)
    flat = context.reshape(rows_dev * cols_dev, width)
    attended = jnp.dot(flat, out_weight, preferred_element_type=jnp.float32).astype(jnp.bfloat16)
    return attended.reshape(rows_dev, cols_dev, width)


def solution(mesh):
    in_specs = (P("row", "col", None), P("row", "col", None), P("row", "col", None), P())
    out_specs = P("row", "col", None)
    return jax.shard_map(body, mesh=mesh, in_specs=in_specs, out_specs=out_specs, check_vma=False)
```

```python
import jax
import jax.numpy as jnp
from jax import lax
from jax.experimental import pallas as pl
from jax.experimental.pallas import tpu as pltpu
from jax.sharding import PartitionSpec as P

HEADS = 8
HEAD_DIM = 128
SCALE = HEAD_DIM**-0.5
BATCHES = 4
PER = 4 // BATCHES
GROUPS = 2 + BATCHES
BLOCK = 256
MASKED = -1e30
RELAYED = 2
WAY = -4
MESH = pl.DeviceIdType.MESH
NT = (((1,), (1,)), ((), ()))


def device(x, y, z, core):
    return (y * 8 + lax.rem(z, 4) * 2 + core, x * 4 + lax.div(z, 4))


NEAREST = (0, 1, 7, 2, 6, 3, 5, 4)


def loop(first, last, step, unroll=1):
    def run(i, carry):
        step(i)
        return carry

    lax.fori_loop(first, last, run, 0, unroll=unroll)


def widen(source, target, per):
    def one(block):
        of_z, of_me = lax.div(block, 8), lax.rem(block, 8)
        piece = source[lax.div(of_me, 2), of_z, lax.rem(of_me, 2)]
        target[pl.ds(pl.multiple_of(block * per * 32, 32), per * 32)] = piece.astype(jnp.float32).reshape(
            per * 32, 128
        )

    loop(0, 32, one, 4)


def by_column(source, wide, target):
    widen(source, wide, 4)

    def one(c):
        target[c] = wide[pl.ds(c, 128, stride=32), :].astype(jnp.bfloat16)

    loop(0, 32, one, 16)


def row_item(query_ref, key_ref, value_ref, part_ref, level_ref, step):
    causal = lax.broadcasted_iota(jnp.int32, (BLOCK, BLOCK), 0) >= lax.broadcasted_iota(
        jnp.int32, (BLOCK, BLOCK), 1
    )
    first = (lax.broadcasted_iota(jnp.int32, (16, 128), 1) == 0).astype(jnp.bfloat16)
    for at in range(1024 // BLOCK):
        here, upto = pl.ds(at * BLOCK, BLOCK), pl.ds(0, (at + 1) * BLOCK)
        scores = lax.dot_general(query_ref[here], key_ref[upto], NT, preferred_element_type=jnp.float32)
        last = jnp.where(causal, scores[:, at * BLOCK :], MASKED)
        scores = jnp.concatenate([scores[:, : at * BLOCK], last], axis=1) if at else last
        best = jnp.max(scores, axis=1, keepdims=True)
        weights = jnp.exp((scores - best) * SCALE)
        total = jnp.maximum(jnp.sum(weights, axis=1, keepdims=True), 1.0)
        summed = jnp.dot(weights.astype(jnp.bfloat16), value_ref[upto], preferred_element_type=jnp.float32)
        part_ref[here] = (summed * (1.0 / total)).astype(jnp.bfloat16)
        level = jnp.broadcast_to(best * SCALE + jnp.log(total), (BLOCK, 128)).astype(jnp.bfloat16)
        turned = lax.dot_general(first, level, NT, preferred_element_type=jnp.float32)
        level_ref[step:, here] = turned[: level_ref.shape[0] - step]


def col_scores(query_ref, wide, key_by_col, scores, per):
    widen(query_ref, wide, per)

    def one(c):
        query = wide[pl.ds(c, 32 * per, stride=32), :].astype(jnp.bfloat16)
        scores[c] = lax.dot_general(query, key_by_col[c], NT, preferred_element_type=jnp.float32)

    loop(0, 32, one, 16)


def col_weights(scores, weights, inverse, part_ref, batch, per):
    queries = 32 * per
    at = lax.broadcasted_iota(jnp.int32, (queries, 128), 0)
    lane = lax.broadcasted_iota(jnp.int32, (queries, 128), 1)

    def grid_row(block, r):
        return lax.div(lax.rem(block, 8), 2) * 32 + lax.div(block, 8) * 8 + lax.rem(block, 2) * 4 + r

    lower = grid_row(lax.div(at, per), batch * per + lax.rem(at, per)) > grid_row(lax.div(lane, 4), lax.rem(lane, 4))

    def one(c, levels):
        masked = jnp.where(lower, scores[c], MASKED)
        best = jnp.max(masked, axis=1, keepdims=True)
        weight = jnp.where(lower, jnp.exp((masked - best) * SCALE), 0.0)
        total = jnp.maximum(jnp.sum(weight, axis=1, keepdims=True), 1.0)
        weights[c] = weight.astype(jnp.bfloat16)
        inverse[c] = jnp.broadcast_to(1.0 / total, (queries, 128))
        return jnp.where(lane == c, best * SCALE + jnp.log(total), levels)

    levels = lax.fori_loop(0, 32, one, jnp.zeros((queries, 128), jnp.float32), unroll=16)
    if queries < 128:
        levels = jnp.concatenate([levels, jnp.zeros((128 - queries, 128), jnp.float32)], axis=0)
    level = levels.T[:32].astype(jnp.bfloat16)
    for of_me in range(8):
        part_ref[of_me // 2, 4, of_me % 2, 0] = level


def col_sums(weights, inverse, value_by_col, wide, part_ref, per):
    def one(c):
        summed = jnp.dot(weights[c], value_by_col[c], preferred_element_type=jnp.float32)
        wide[pl.ds(c, 32 * per, stride=32), :] = summed * inverse[c]

    loop(0, 32, one, 16)

    def narrow(block):
        of_z, of_me = lax.div(block, 8), lax.rem(block, 8)
        piece = wide[pl.ds(pl.multiple_of(block * per * 32, 32), per * 32)]
        part_ref[lax.div(of_me, 2), of_z, lax.rem(of_me, 2)] = piece.astype(jnp.bfloat16).reshape(per, 32, 128)

    loop(0, 32, narrow, 4)


def combine(row_levels, row_parts, col_levels, col_parts, contexts, batch, shift, per):
    stacked = jnp.concatenate([row_levels[source] for source in range(4)], axis=0)
    if 32 * per < 128:
        stacked = jnp.concatenate([stacked, jnp.zeros((128 - 32 * per, 256), jnp.float32)], axis=0)
    row_level = stacked.T
    col_level = pltpu.roll(col_levels[...].astype(jnp.float32), shift, 1)
    top = jnp.maximum(row_level, col_level)
    row_factor = jnp.exp(row_level - top)
    col_factor = jnp.exp(col_level - top)
    inverse = 1.0 / (row_factor + col_factor)
    row_factor, col_factor = row_factor * inverse, col_factor * inverse
    for source in range(4):
        for step in range(per):
            lane = source * 8 * per + step
            r = batch * per + step
            contexts[source, r] = (
                row_factor[:, lane : lane + 1] * row_parts[source, r].astype(jnp.float32)
                + col_factor[:, lane : lane + 1] * col_parts[source, r].astype(jnp.float32)
            ).astype(jnp.bfloat16)


def kernel(
    q_in,
    k_in,
    v_in,
    out,
    home_q,
    home_k,
    home_v,
    row_q,
    row_k,
    row_v,
    col_q,
    col_k,
    col_v,
    row_part,
    row_level,
    col_part,
    home_row_part,
    home_row_level,
    home_col_part,
    home_context,
    key_by_col,
    value_by_col,
    wide,
    wide_q,
    wide_o,
    scores,
    weights,
    inverse,
    in_send,
    in_recv,
    row_send,
    row_recv,
    col_send,
    col_recv,
    row_back_send,
    row_back_recv,
    col_back_send,
    col_back_recv,
    out_send,
    out_recv,
    relay,
    relay_send,
    relay_recv,
):
    at_row, at_col = lax.axis_index("row"), lax.axis_index("col")
    y, z_lo, core = lax.div(at_row, 8), lax.rem(lax.div(at_row, 2), 4), lax.rem(at_row, 2)
    x, z_hi = lax.div(at_col, 4), lax.rem(at_col, 4)
    z = z_hi * 4 + z_lo
    near = lax.div(z, 2)
    active = lax.rem(z, 2) == 0
    me = y * 2 + core
    relaying = jnp.logical_and(active, core == 1)

    def peer_x(other):
        return device(other, y, z, core)

    def peer_yc(other):
        return device(x, lax.div(other, 2), z, lax.rem(other, 2))

    def peer_z(other):
        return device(x, y, other, core)

    def remote(src, dst, send, recv, to):
        return pltpu.make_async_remote_copy(
            src_ref=src, dst_ref=dst, send_sem=send, recv_sem=recv, device_id=to, device_id_type=MESH
        )

    def await_bytes(ref, semaphore):
        pltpu.make_async_copy(ref, ref, semaphore).wait()

    def others(mine, count, step):
        for offset in range(1, count):
            step(lax.rem(mine + offset, count))

    barrier = pltpu.get_barrier_semaphore()

    def greet(to):
        pl.semaphore_signal(barrier, inc=1, device_id=to, device_id_type=MESH)

    @pl.when(active)
    def _():
        others(z, 16, lambda other: greet(peer_z(other)))
        others(x, 4, lambda other: greet(peer_x(other)))
        others(me, 8, lambda other: greet(peer_yc(other)))
        pl.semaphore_wait(barrier, 25)

    @pl.when(jnp.logical_not(active))
    def _():
        for head in range(HEADS):
            greet(peer_z(head * 2))
        pl.semaphore_wait(barrier, 8)

    def rows_of(group):
        return pl.ds(0, 4) if group < 2 else pl.ds((group - 2) * PER, PER)

    def of(group, key, value, query):
        return (key, value)[group] if group < 2 else query

    def in_copy(group, head):
        rows = rows_of(group)
        src = of(group, k_in, v_in, q_in).at[rows, :, pl.ds(pl.multiple_of(head * 128, 128), 128)]
        dst = in_slot(group, z)
        return remote(src, dst, in_send.at[group, head], in_recv.at[group], peer_z(head * 2))

    def in_slot(group, source):
        columns = pl.ds(pl.multiple_of(lax.div(source, 4) * 64, 64), 64)
        return of(group, home_k, home_v, home_q).at[lax.rem(source, 4), rows_of(group), columns, :]

    def relay_in(group):
        src = (k_in, v_in)[group].at[:, :, pl.ds(pl.multiple_of(lax.rem(near + 4, 8) * 128, 128), 128)]
        return remote(
            src,
            relay.at[group],
            in_send.at[group, lax.rem(near + 4, 8)],
            relay_recv.at[group],
            peer_z(lax.rem(z + 16 + WAY, 16)),
        )

    def relay_on(group):
        return remote(
            relay.at[group],
            in_slot(group, lax.rem(z + 16 - WAY, 16)),
            relay_send.at[group],
            in_recv.at[group],
            peer_z(lax.rem(z + 16 + WAY, 16)),
        )

    def relay_forward(group):
        @pl.when(relaying)
        def _():
            await_bytes(relay.at[group], relay_recv.at[group])
            relay_on(group).start()

    def in_own(group):
        src = of(group, k_in, v_in, q_in).at[rows_of(group), :, pl.ds(pl.multiple_of(near * 128, 128), 128)]
        return pltpu.make_async_copy(src, in_slot(group, z), in_recv.at[group])

    def in_step(group, offset, before):
        head = lax.rem(near + offset, 8)

        def go():
            if before is not None:
                in_copy(before, head).wait_send()
            if group is None:
                return
            if offset == 4 and group < RELAYED:

                @pl.when(relaying)
                def _():
                    relay_in(group).start()

                @pl.when(jnp.logical_not(relaying))
                def _():
                    in_copy(group, head).start()

            else:
                in_copy(group, head).start()

        if offset:
            go()
        else:

            @pl.when(active)
            def _():
                if group is not None:
                    in_own(group).start()

            @pl.when(jnp.logical_not(active))
            def _():
                go()

    def in_start(group):
        for offset in reversed(NEAREST):
            in_step(group, offset, None)

    def in_next(group):
        for offset in NEAREST:
            in_step(group + 1, offset, group)

    def in_sent(group):
        for offset in NEAREST:
            in_step(None, offset, group)

    def in_wait(group):
        await_bytes(of(group, home_k, home_v, home_q).at[:, rows_of(group)], in_recv.at[group])

    def row_slot(group, source):
        columns = pl.ds(pl.multiple_of(source * 256, 256), 256)
        return of(group, row_k, row_v, row_q).at[rows_of(group), columns, :]

    def row_copy(group, other):
        src = of(group, home_k, home_v, home_q).at[other, rows_of(group)]
        return remote(src, row_slot(group, x), row_send.at[group], row_recv.at[group], peer_x(other))

    def row_own(group):
        src = of(group, home_k, home_v, home_q).at[x, rows_of(group)]
        return pltpu.make_async_copy(src, row_slot(group, x), row_recv.at[group])

    def row_wait(group):
        await_bytes(of(group, row_k, row_v, row_q).at[rows_of(group)], row_recv.at[group])

    def col_slot(group, source):
        of_y, of_core = lax.div(source, 2), lax.rem(source, 2)
        if group < 2:
            return (col_k, col_v)[group].at[of_y, :, of_core]
        return col_q.at[group - 2, of_y, :, of_core]

    def col_source(group, other):
        columns = pl.ds(pl.multiple_of(other * 32, 32), 32)
        return of(group, home_k, home_v, home_q).at[:, rows_of(group), columns, :]

    def col_copy(group, other):
        return remote(
            col_source(group, other), col_slot(group, me), col_send.at[group], col_recv.at[group], peer_yc(other)
        )

    def col_own(group):
        return pltpu.make_async_copy(col_source(group, me), col_slot(group, me), col_recv.at[group])

    def col_wait(group):
        await_bytes((col_k, col_v)[group] if group < 2 else col_q.at[group - 2], col_recv.at[group])

    def spread(group):
        others(x, 4, lambda other: row_copy(group, other).start())
        others(me, 8, lambda other: col_copy(group, other).start())
        row_own(group).start()
        col_own(group).start()

    def spread_sent(group):
        home = of(group, home_k, home_v, home_q)
        await_bytes(home.at[pl.ds(0, 3), rows_of(group)], row_send.at[group])
        await_bytes(home.at[:, rows_of(group), pl.ds(0, 224), :], col_send.at[group])

    def row_back(batch, other, copy):
        rows = pl.ds(batch * PER, PER)
        columns = pl.ds(pl.multiple_of(other * 256, 256), 256)
        copy(
            row_part.at[rows, columns, :],
            home_row_part.at[x, rows],
            row_back_send.at[batch, 0],
            row_back_recv.at[batch, 0],
        )
        copy(
            row_level.at[batch, :, columns],
            home_row_level.at[batch, x],
            row_back_send.at[batch, 1],
            row_back_recv.at[batch, 1],
        )

    def col_back(batch, other, copy):
        copy(
            col_part.at[batch, lax.div(other, 2), :, lax.rem(other, 2)],
            home_col_part.at[:, pl.ds(batch * PER, PER), pl.ds(pl.multiple_of(me * 32, 32), 32), :],
            col_back_send.at[batch],
            col_back_recv.at[batch],
        )

    def send_to(device_id):
        return lambda src, dst, send, recv: remote(src, dst, send, recv, device_id).start()

    def keep(src, dst, send, recv):
        pltpu.make_async_copy(src, dst, recv).start()

    def row_return(batch):
        others(x, 4, lambda other: row_back(batch, other, send_to(peer_x(other))))
        row_back(batch, x, keep)

    def col_return(batch):
        others(me, 8, lambda other: col_back(batch, other, send_to(peer_yc(other))))
        col_back(batch, me, keep)

    def return_wait(batch):
        rows = pl.ds(batch * PER, PER)
        await_bytes(home_row_part.at[:, rows], row_back_recv.at[batch, 0])
        await_bytes(home_row_level.at[batch], row_back_recv.at[batch, 1])
        await_bytes(home_col_part.at[:, rows], col_back_recv.at[batch])

    def return_sent(batch):
        rows = pl.ds(batch * PER, PER)
        await_bytes(row_part.at[rows, pl.ds(0, 768), :], row_back_send.at[batch, 0])
        await_bytes(row_level.at[batch, :, pl.ds(0, 768)], row_back_send.at[batch, 1])
        await_bytes(home_col_part.at[:, rows, pl.ds(0, 224), :], col_back_send.at[batch])

    def out_slot(batch, head):
        return out.at[pl.ds(batch * PER, PER), :, pl.ds(pl.multiple_of(head * 128, 128), 128)]

    def out_source(batch, other):
        columns = pl.ds(pl.multiple_of(lax.div(other, 4) * 64, 64), 64)
        return home_context.at[lax.rem(other, 4), pl.ds(batch * PER, PER), columns, :]

    def out_copy(batch, other):
        return remote(
            out_source(batch, other), out_slot(batch, near), out_send.at[batch], out_recv.at[batch], peer_z(other)
        )

    def out_start(batch):
        others(z, 16, lambda other: out_copy(batch, other).start())
        pltpu.make_async_copy(out_source(batch, z), out_slot(batch, near), out_recv.at[batch]).start()

    def out_sent(batch):
        await_bytes(row_part.at[pl.ds(batch * PER, PER), pl.ds(0, 960), :], out_send.at[batch])

    def out_arrived(batch):
        await_bytes(out.at[pl.ds(batch * PER, PER)], out_recv.at[batch])

    def row_work(batch):
        row_wait(2 + batch)
        for step in range(PER):
            r = batch * PER + step
            row_item(row_q.at[r], row_k.at[r], row_v.at[r], row_part.at[r], row_level.at[batch], step)
        row_return(batch)

    def col_work(batch):
        col_wait(2 + batch)
        col_scores(col_q.at[batch], wide_q, key_by_col, scores, PER)
        col_weights(scores, weights, inverse, col_part.at[batch], batch, PER)
        col_sums(weights, inverse, value_by_col, wide_o, col_part.at[batch], PER)
        col_return(batch)

    def finish(batch):
        return_wait(batch)
        combine(
            home_row_level.at[batch],
            home_row_part,
            home_col_part.at[4, batch * PER],
            home_col_part,
            home_context,
            batch,
            lax.rem(128 - me * PER, 128),
            PER,
        )
        out_start(batch)

    in_start(0)
    for group in range(2):
        in_next(group)

        @pl.when(active)
        def _(group=group):
            relay_forward(group)
            in_wait(group)
            spread(group)
            if group == 0:
                col_wait(0)
                by_column(col_k, wide, key_by_col)

    for batch in range(BATCHES):
        if batch + 1 < BATCHES:
            in_next(2 + batch)

        @pl.when(active)
        def _(batch=batch):
            in_wait(2 + batch)
            spread(2 + batch)
            if batch == 3:
                finish(0)
            if batch == 1:
                col_wait(1)
                by_column(col_v, wide, value_by_col)
                row_wait(0)
                row_wait(1)
            if batch > 0:
                row_work(batch - 1)
                col_work(batch - 1)

    @pl.when(active)
    def _():
        finish(1)
        row_work(BATCHES - 1)
        col_work(BATCHES - 1)
        finish(BATCHES - 2)
        finish(BATCHES - 1)
        for group in range(GROUPS):
            spread_sent(group)

        @pl.when(relaying)
        def _():
            for group in range(RELAYED):
                await_bytes(relay.at[group], relay_send.at[group])

        for batch in range(BATCHES):
            return_sent(batch)
            out_sent(batch)

    in_sent(GROUPS - 1)
    for batch in range(BATCHES):
        out_arrived(batch)


def attention(queries, key_vectors, values):
    bf16, f32 = jnp.bfloat16, jnp.float32
    dma = pltpu.SemaphoreType.DMA
    home = pltpu.VMEM((4, 4, 256, 128), bf16)
    rows = pltpu.VMEM((4, 1024, 128), bf16)
    columns = pltpu.VMEM((4, 4, 2, 4, 32, 128), bf16)
    anywhere = pl.BlockSpec(memory_space=pl.ANY)
    return pl.pallas_call(
        kernel,
        out_shape=jax.ShapeDtypeStruct(queries.shape, bf16),
        in_specs=[anywhere] * 3,
        out_specs=anywhere,
        scratch_shapes=[
            home,
            home,
            home,
            rows,
            rows,
            rows,
            pltpu.VMEM((BATCHES, 4, 4, 2, PER, 32, 128), bf16),
            columns,
            columns,
            rows,
            pltpu.VMEM((BATCHES, 8 * PER, 1024), f32),
            pltpu.VMEM((BATCHES, 4, 5, 2, PER, 32, 128), bf16),
            home,
            pltpu.VMEM((BATCHES, 4, 8 * PER, 256), f32),
            pltpu.VMEM((5, 4, 256, 128), bf16),
            home,
            pltpu.VMEM((32, 128, 128), bf16),
            pltpu.VMEM((32, 128, 128), bf16),
            pltpu.VMEM((4096, 128), f32),
            pltpu.VMEM((32 * PER * 32, 128), f32),
            pltpu.VMEM((32 * PER * 32, 128), f32),
            pltpu.VMEM((32, 32 * PER, 128), f32),
            pltpu.VMEM((32, 32 * PER, 128), bf16),
            pltpu.VMEM((32, 32 * PER, 128), f32),
            dma((GROUPS, 8)),
            dma((GROUPS,)),
            dma((GROUPS,)),
            dma((GROUPS,)),
            dma((GROUPS,)),
            dma((GROUPS,)),
            dma((BATCHES, 2)),
            dma((BATCHES, 2)),
            dma((BATCHES,)),
            dma((BATCHES,)),
            dma((BATCHES,)),
            dma((BATCHES,)),
            pltpu.VMEM((RELAYED, 4, 64, 128), bf16),
            dma((RELAYED,)),
            dma((RELAYED,)),
        ],
        compiler_params=pltpu.CompilerParams(
            collective_id=0, has_side_effects=True, vmem_limit_bytes=60 * 1024 * 1024
        ),
    )(queries, key_vectors, values)


def body(queries, key_vectors, values, out_weight):
    rows_dev, cols_dev, width = queries.shape
    context = attention(queries, key_vectors, values)
    flat = context.reshape(rows_dev * cols_dev, width)
    attended = jnp.dot(flat, out_weight, preferred_element_type=jnp.float32).astype(jnp.bfloat16)
    return attended.reshape(rows_dev, cols_dev, width)


def solution(mesh):
    in_specs = (P("row", "col", None), P("row", "col", None), P("row", "col", None), P())
    out_specs = P("row", "col", None)
    return jax.shard_map(body, mesh=mesh, in_specs=in_specs, out_specs=out_specs, check_vma=False)
```
